32 devices in a mesh: grp: 2 (over y), row: 4 (over z), col: 2 (over x), chan: 2 (over core).
Axes of the slice: x: 2, y: 2, z: 4, core: 2. Of those that a mesh axis runs over, the one named last changes fastest.
Arguments:
- pair: bfloat16 [128, 64, 128], P(('grp', 'row'), 'col'), parts along dimension 0, may hold values from -6 to 6
- window_start: int32 [2], P('grp'), parts along dimension 0, may hold values from 0 to 960
- residue_mask: int32 [2048], P('grp'), parts along dimension 0, may hold values 0 or 1
- in_gain: float32 [2, 128], replicated, may hold values from 0.25 to 1.75
- in_proj: bfloat16 [2, 128, 4, 128], P(None, None, None, 'chan'), may hold values from -0.5 to 0.5
- gate_proj: bfloat16 [2, 128, 128], replicated, may hold values from -0.5 to 0.5
- out_gain: float32 [2, 128], replicated, may hold values from 0.25 to 1.75
- out_proj: bfloat16 [2, 128, 128], replicated, may hold values from -0.5 to 0.5
- cotangent: bfloat16 [128, 64, 128], P(('grp', 'row'), ('col', 'chan')), parts along dimension 0, may hold values from -6 to 6
Outputs:
- new_pair: bfloat16 [128, 64, 128], P(('grp', 'row'), ('col', 'chan')), parts along dimension 0
- pair_grad: float32 [128, 64, 128], P(('grp', 'row'), ('col', 'chan')), parts along dimension 0
The draws below stay inside these ranges and needn't reach their ends.
There are 2 independent parts, one for each index of `grp`. The reference program is written for one: setup_inputs(seed, part) draws one part's arguments, and reference() takes and returns one part's arrays. A program takes and returns all parts, laid end to end along the dimension named above; an argument that names none is the same for every part. Nothing has to cross between parts.
Inputs may be any that keep to these rules, and one draw needn't show every extreme that they name: The window of 64 residues from window_start lies inside the complex.
All inputs are finite; a program needn't handle non-finite values.
Results may differ from the reference program's by a relative error of at most 0.013.
Values may be sent and summed in bfloat16 or wider, within the bound.
A program may use at most 64 MiB of HBM per device.

```python
import jax
import jax.numpy as jnp
from jax import lax

C = 128
H = 128
N = 64
FULL = 1024
N_ROW = 4
N_COL = 2


def set_ends(values, stream_key, least, largest):
    place = [jax.random.randint(jax.random.fold_in(stream_key, axis), (), 0, length) for axis, length in enumerate(values.shape)]
    main_axis = values.shape.index(max(values.shape))
    neighbour = place[:main_axis] + [(place[main_axis] + 1) % values.shape[main_axis]] + place[main_axis + 1:]
    return values.at[tuple(place)].set(least).at[tuple(neighbour)].set(largest)


def steps_of(rng, dims, split, smallest, largest):
    factor_of, own = 1.0, jax.random.fold_in(rng, 6)
    for dim, parts in split:
        steps = jnp.exp(jax.random.uniform(jax.random.fold_in(own, dim), (parts,), jnp.float32, smallest / len(split), largest / len(split)))
        factor_of = factor_of * jnp.repeat(steps, dims[dim] // parts).reshape([-1 if axis == dim else 1 for axis in range(len(dims))])
    return factor_of


def gaussian(stream_key, dims, deviation, most, split=(), dtype=jnp.bfloat16):
    entries = jax.random.normal(stream_key, dims, jnp.float32) * deviation
    if len(split) > 0:
        entries = steps_of(stream_key, dims, split, -0.22, 0.18) * entries
    return jnp.clip(entries, min=-most, max=most).astype(dtype)


def setup_inputs(seed: int = 0, part: int = 0) -> dict:
    key_list = jax.random.split(jax.random.key(seed), 10)
    part_splits = jax.random.split(jax.random.fold_in(key_list[9], part), 10)
    return {
        "pair": gaussian(part_splits[0], (N, N, C), 1.0, 6.0, ((0, 4), (1, 2))),
        "window_start": jax.random.randint(part_splits[1], (1,), 0, FULL - N + 1).astype(jnp.int32),
        "residue_mask": set_ends((jax.random.randint(part_splits[2], (FULL,), 0, 4) < 3).astype(jnp.int32), jax.random.fold_in(part_splits[2], 1), 0, 1),
        "in_gain": jnp.clip(1.0 + 0.15 * jax.random.normal(key_list[3], (2, C), jnp.float32), 0.25, 1.75),
        "in_proj": gaussian(key_list[4], (2, C, 4, H), C ** -0.5, 0.5, ((3, 2),)),
        "gate_proj": gaussian(key_list[5], (2, C, C), C ** -0.5, 0.5),
        "out_gain": jnp.clip(1.0 + 0.15 * jax.random.normal(key_list[6], (2, H), jnp.float32), 0.25, 1.75),
        "out_proj": gaussian(key_list[7], (2, H, C), H ** -0.5, 0.5),
        "cotangent": gaussian(part_splits[8], (N, N, C), 1.0, 6.0, ((0, 4), (1, 4))),
    }


def rounded(values):
    return lax.optimization_barrier(values.astype(jnp.bfloat16)).astype(jnp.float32)

def layer_norm(values, norm_gain):
    center = values - lax.optimization_barrier(jnp.mean(values, axis=-1, keepdims=True))
    spread = lax.optimization_barrier(jnp.mean(center * center, axis=-1, keepdims=True))
    return center * lax.rsqrt(spread + 1e-05) * norm_gain

def gated_half(projected, pair_mask):
    return jax.nn.sigmoid(projected[0]) * projected[1] * pair_mask

def gated_pair(projected, pair_mask):
    return (gated_half(projected[0:2], pair_mask), gated_half(projected[2:4], pair_mask))

def project_pair(tile_values, norm_gain, weight):
    normed = rounded(layer_norm(tile_values.astype(jnp.float32), norm_gain))
    return jnp.einsum('ijc,cgh->ghij', normed, weight.astype(jnp.float32), precision=lax.Precision.HIGHEST)

def finish_update(hidden, current, norm_gain, gate_weight, hidden_gain, out_weight):
    normed = rounded(layer_norm(current, norm_gain))
    gate = jax.nn.sigmoid(jnp.einsum('ijc,cd->ijd', normed, gate_weight.astype(jnp.float32), precision=lax.Precision.HIGHEST))
    scaled = rounded(layer_norm(hidden, hidden_gain))
    update = jnp.einsum('ijh,hc->ijc', scaled, out_weight.astype(jnp.float32), precision=lax.Precision.HIGHEST)
    return (current + gate * update, gate, update)

def finish_backward(hidden, current, norm_gain, gate_weight, hidden_gain, out_weight, grad, gate, update):
    d_update = grad * gate
    d_logit = grad * update * gate * (1.0 - gate)
    d_scaled = jnp.einsum('ijc,hc->ijh', d_update, out_weight.astype(jnp.float32), precision=lax.Precision.HIGHEST)
    d_normed = jnp.einsum('ijd,cd->ijc', d_logit, gate_weight.astype(jnp.float32), precision=lax.Precision.HIGHEST)
    _, back_hidden = jax.vjp(lambda values: layer_norm(values, hidden_gain), hidden)
    _, back_current = jax.vjp(lambda values: layer_norm(values, norm_gain), current)
    d_hidden, = back_hidden(d_scaled)
    d_current, = back_current(d_normed)
    return (rounded(d_hidden), grad + d_current)

def entry_backward(tile_values, norm_gain, weight, projected, pair_mask, d_left, d_right):
    _, back_gate = jax.vjp(lambda values: gated_pair(values, pair_mask), projected)
    d_projected, = back_gate((d_left, d_right))
    d_entry = jnp.einsum('ghij,cgh->ijc', d_projected, weight.astype(jnp.float32), precision=lax.Precision.HIGHEST)
    _, back_norm = jax.vjp(lambda values: layer_norm(values, norm_gain), tile_values.astype(jnp.float32))
    d_tile, = back_norm(d_entry)
    return d_tile

def reference(pair, window_start, residue_mask, in_gain, in_proj, gate_proj, out_gain, out_proj, cotangent):
    high = lax.Precision.HIGHEST
    window_mask = lax.dynamic_slice_in_dim(residue_mask, window_start[0], N).astype(jnp.float32)
    pair_mask = window_mask[:, None] * window_mask[None, :]
    pair_value = pair.astype(jnp.float32)
    col_extent = N // N_COL
    row_extent = N // N_ROW
    projected_zero = project_pair(pair_value, in_gain[0], in_proj[0])
    left_zero, right_zero = gated_pair(projected_zero, pair_mask)
    left_zero = rounded(left_zero)
    right_zero = rounded(right_zero)
    hidden_zero = jnp.zeros((N, N, H), jnp.float32)
    for segment in range(N_COL):
        lower = segment * col_extent
        partial_sum = jnp.einsum('hik,hjk->ijh', left_zero[:, :, lower:lower + col_extent], right_zero[:, :, lower:lower + col_extent], precision=high)
        hidden_zero = hidden_zero + rounded(partial_sum)
    hidden_zero = rounded(hidden_zero)
    middle_f, gate_zero, update_zero = finish_update(hidden_zero, pair_value, in_gain[0], gate_proj[0], out_gain[0], out_proj[0])
    middle = rounded(middle_f)
    projected_one = project_pair(middle, in_gain[1], in_proj[1])
    left_one, right_one = gated_pair(projected_one, pair_mask)
    left_one = rounded(left_one)
    right_one = rounded(right_one)
    hidden_one = jnp.zeros((N, N, H), jnp.float32)
    for segment in range(N_ROW):
        lower = segment * row_extent
        partial_sum = jnp.einsum('hki,hkj->ijh', left_one[:, lower:lower + row_extent, :], right_one[:, lower:lower + row_extent, :], precision=high)
        hidden_one = hidden_one + rounded(partial_sum)
    hidden_one = rounded(hidden_one)
    final_f, gate_one, update_one = finish_update(hidden_one, middle, in_gain[1], gate_proj[1], out_gain[1], out_proj[1])
    new_pair = final_f.astype(jnp.bfloat16)
    grad_two = cotangent.astype(jnp.float32)
    d_hidden_one, direct_one = finish_backward(hidden_one, middle, in_gain[1], gate_proj[1], out_gain[1], out_proj[1], grad_two, gate_one, update_one)
    d_right_one = jnp.einsum('hki,ijh->hkj', left_one, d_hidden_one, precision=high)
    d_left_one = jnp.zeros((H, N, N), jnp.float32)
    for segment in range(N_COL):
        lower = segment * col_extent
        partial_sum = jnp.einsum('hkj,ijh->hki', right_one[:, :, lower:lower + col_extent], d_hidden_one[:, lower:lower + col_extent, :], precision=high)
        d_left_one = d_left_one + rounded(partial_sum)
    grad_one = direct_one + entry_backward(middle, in_gain[1], in_proj[1], projected_one, pair_mask, d_left_one, d_right_one)
    d_hidden_zero, direct_zero = finish_backward(hidden_zero, pair_value, in_gain[0], gate_proj[0], out_gain[0], out_proj[0], grad_one, gate_zero, update_zero)
    d_left_zero = jnp.einsum('ijh,hjk->hik', d_hidden_zero, right_zero, precision=high)
    d_right_zero = jnp.zeros((H, N, N), jnp.float32)
    for segment in range(N_ROW):
        lower = segment * row_extent
        partial_sum = jnp.einsum('ijh,hik->hjk', d_hidden_zero[lower:lower + row_extent], left_zero[:, lower:lower + row_extent, :], precision=high)
        d_right_zero = d_right_zero + rounded(partial_sum)
    pair_grad = direct_zero + entry_backward(pair_value, in_gain[0], in_proj[0], projected_zero, pair_mask, d_left_zero, d_right_zero)
    return (new_pair, pair_grad)
```

```python
import functools

import jax
import jax.numpy as jnp
from jax import lax
from jax.experimental import pallas as pl
from jax.experimental.pallas import tpu as pltpu
from jax.sharding import PartitionSpec as P

F32 = jnp.float32
BF16 = jnp.bfloat16
MESH = pl.DeviceIdType.MESH

A0_ROW, B0_TOQ, A0_COL, B0_COL, B1_COL, A1_TOR, A1_ROW, B1_ROW = range(8)
D1_COL, D1_TOQ, D0_ROW, D0_TOR = range(8, 12)
KINDS = 12


def dot(a, b):
    return lax.dot_general(a, b, (((1,), (0,)), ((), ())), preferred_element_type=F32)


def dot_t(a, b):
    return lax.dot_general(a, b, (((1,), (1,)), ((), ())), preferred_element_type=F32)


def unit(x):
    center = x - jnp.mean(x, axis=-1, keepdims=True)
    inv = lax.rsqrt(jnp.mean(center * center, axis=-1, keepdims=True) + 1e-05)
    return center * inv, inv


def unit_back(hat, inv, d_hat):
    mean = jnp.mean(d_hat, axis=-1, keepdims=True)
    slope = jnp.mean(d_hat * hat, axis=-1, keepdims=True)
    return inv * (d_hat - mean - hat * slope)


def kernel(
    n,
    n_chan,
    pair_ref,
    start_ref,
    residue_ref,
    in_gain_ref,
    in_proj_ref,
    gate_proj_ref,
    out_gain_ref,
    out_proj_ref,
    cot_ref,
    new_ref,
    grad_ref,
    buf,
    stage,
    weight,
    mask_ref,
    lhs_ref,
    acc_ref,
    proj_ref,
    wide_ref,
    send_sem,
    recv_sem,
    weight_send,
    weight_recv,
):
    t = pair_ref.shape[0]
    ch = pair_ref.shape[2]
    hid = weight.shape[2]
    cells = t * t
    r = lax.axis_index("row")
    chan = lax.axis_index("chan")
    q = lax.axis_index("col") * n_chan + chan
    same = r == q

    def at(row, place):
        return {"row": row, "col": place // n_chan, "chan": lax.rem(place, n_chan)}

    def targets(way):
        if way == "row":
            return [(at(r, lax.rem(q + d, n)), False) for d in range(1, n)]
        if way == "col":
            return [(at(lax.rem(r + d, n), q), False) for d in range(1, n)]
        if way == "to_q":
            return [(at(lax.rem(r + d, n), r), d == 0) for d in range(n)]
        return [(at(q, lax.rem(q + d, n)), d == 0) for d in range(n)]

    ways = {
        A0_ROW: "row",
        A1_ROW: "row",
        B1_ROW: "row",
        D0_ROW: "row",
        A0_COL: "col",
        B0_COL: "col",
        B1_COL: "col",
        D1_COL: "col",
        B0_TOQ: "to_q",
        D1_TOQ: "to_q",
        A1_TOR: "to_r",
        D0_TOR: "to_r",
    }

    barrier = pltpu.get_barrier_semaphore()
    for way in ("row", "col", "to_q", "to_r"):
        for device, maybe_self in targets(way):

            def greet(device=device):
                pl.semaphore_signal(barrier, inc=1, device_id=device, device_id_type=MESH)

            if maybe_self:
                pl.when(jnp.logical_not(same))(greet)
            else:
                greet()
    count = 4 * n - 2

    @pl.when(same)
    def _():
        pl.semaphore_wait(barrier, count - 2)

    @pl.when(jnp.logical_not(same))
    def _():
        pl.semaphore_wait(barrier, count)

    def slot_of(kind):
        return q if ways[kind] in ("row", "to_q") else r

    pending = []

    def push(kind, source):
        slot = slot_of(kind)
        for step, (device, maybe_self) in enumerate(targets(ways[kind])):
            copy = pltpu.make_async_remote_copy(
                src_ref=source,
                dst_ref=buf.at[kind, slot],
                send_sem=send_sem.at[kind, step],
                recv_sem=recv_sem.at[kind, slot],
                device_id=device,
                device_id_type=MESH,
            )
            pending.append((copy, maybe_self))
            if maybe_self:
                pl.when(jnp.logical_not(same))(copy.start)
            else:
                copy.start()

    def arrive(kind, slot):
        copy = pltpu.make_async_remote_copy(
            src_ref=buf.at[kind, slot],
            dst_ref=buf.at[kind, slot],
            send_sem=send_sem.at[kind, 0],
            recv_sem=recv_sem.at[kind, slot],
            device_id={"row": r},
            device_id_type=MESH,
        )
        way = ways[kind]
        if way in ("row", "col"):
            pl.when(slot != (q if way == "row" else r))(copy.wait_recv)
        else:
            pl.when(jnp.logical_not(jnp.logical_and(same, slot == r)))(copy.wait_recv)

    part = in_proj_ref.shape[2]
    mine = pl.ds(pl.multiple_of(chan * part, part), part)
    weight_copies = []
    for u in range(2):
        for d in range(1, n_chan):
            copy = pltpu.make_async_remote_copy(
                src_ref=in_proj_ref.at[u],
                dst_ref=weight.at[u, :, mine, :],
                send_sem=weight_send.at[u, d - 1],
                recv_sem=weight_recv.at[u, chan],
                device_id={"chan": lax.rem(chan + d, n_chan)},
                device_id_type=MESH,
            )
            copy.start()
            weight_copies.append(copy)
    weight[:, :, mine, :] = in_proj_ref[...]

    first = start_ref[0]
    rows = lax.broadcasted_iota(jnp.int32, (t, ch), 0)
    col_mask = jnp.zeros((t, ch), F32)
    for j in range(t):
        value = residue_ref[first + q * t + j].astype(F32)
        col_mask = jnp.where(rows == j, value, col_mask)
    for i in range(t):
        mask_ref[i] = col_mask * residue_ref[first + r * t + i].astype(F32)

    def wait_weight(u):
        for d in range(1, n_chan):
            other = lax.rem(chan + d, n_chan)
            theirs = pl.ds(pl.multiple_of(other * part, part), part)
            pltpu.make_async_remote_copy(
                src_ref=in_proj_ref.at[u],
                dst_ref=weight.at[u, :, theirs, :],
                send_sem=weight_send.at[u, d - 1],
                recv_sem=weight_recv.at[u, other],
                device_id={"chan": other},
                device_id_type=MESH,
            ).wait_recv()

    def enter(u, x):
        hat, inv = unit(x)
        normed = (hat * in_gain_ref[u : u + 1, :]).astype(BF16)
        wide = weight[u].reshape(4 * hid, ch)
        proj_ref[u] = dot_t(normed, wide)
        mask = mask_ref[...].reshape(cells, ch)
        left = jax.nn.sigmoid(proj_ref[u, :, 0:hid]) * proj_ref[u, :, hid : 2 * hid] * mask
        right = (
            jax.nn.sigmoid(proj_ref[u, :, 2 * hid : 3 * hid])
            * proj_ref[u, :, 3 * hid : 4 * hid]
            * mask
        )
        return hat, inv, normed, left, right

    def gate_of(u, normed):
        return jax.nn.sigmoid(dot(normed, gate_proj_ref[u]))

    def product(left_kind, right_kind, left_major, start):
        acc_ref[...] = jnp.zeros_like(acc_ref)

        def body(d, carry):
            s = lax.rem(start + d, n)
            arrive(left_kind, s)
            arrive(right_kind, s)
            lhs_ref[...] = buf[left_kind, s].astype(F32)
            for low in range(0, t, 8):
                acc = acc_ref[low : low + 8]
                for k in range(t):
                    right = buf[right_kind, s, k].astype(F32)
                    if left_major:
                        left = lhs_ref[low : low + 8, k : k + 1, :]
                    else:
                        left = lhs_ref[k, low : low + 8, :].reshape(8, 1, hid)
                    acc = acc + left * right[None]
                acc_ref[low : low + 8] = acc
            return carry

        lax.fori_loop(0, n, body, 0)
        return acc_ref[...].reshape(cells, hid)

    def drop(kind, slot, value):
        buf[kind, slot] = value

    def finish(u, hidden, x, gate):
        hat, inv = unit(hidden)
        scaled = (hat * out_gain_ref[u : u + 1, :]).astype(BF16)
        update = dot(scaled, out_proj_ref[u])
        return hat, inv, update, x + gate * update

    def leave(u, grad, gate, update, hat, inv):
        d_update = grad * gate
        d_logit = d_update * update * (1.0 - gate)
        d_scaled = dot_t(d_update.astype(BF16), out_proj_ref[u])
        d_hidden = unit_back(hat, inv, d_scaled * out_gain_ref[u : u + 1, :])
        return d_hidden, d_logit

    def entry(u, grad, d_left, d_right, d_normed, hat, inv):
        mask = mask_ref[...].reshape(cells, ch)
        for side, value in ((0, d_left * mask), (2, d_right * mask)):
            gate = jax.nn.sigmoid(proj_ref[u, :, side * hid : (side + 1) * hid])
            held = proj_ref[u, :, (side + 1) * hid : (side + 2) * hid]
            slope = value * gate
            wide_ref[:, side * hid : (side + 1) * hid] = (slope * held * (1.0 - gate)).astype(BF16)
            wide_ref[:, (side + 1) * hid : (side + 2) * hid] = slope.astype(BF16)
        d_entry = dot(wide_ref[...], weight[u].reshape(4 * hid, ch))
        return grad + unit_back(hat, inv, (d_entry + d_normed) * in_gain_ref[u : u + 1, :])

    own = pl.ds(pl.multiple_of(chan * t, t), t)
    x0 = pair_ref[:, own, :].astype(F32).reshape(cells, ch)
    wait_weight(0)
    hat0, inv0, normed0, left, right = enter(0, x0)
    turned = jnp.swapaxes(right.reshape(t, t, hid), 0, 1).astype(BF16)
    stage[0] = turned
    pl.when(same)(lambda: drop(B0_TOQ, q, turned))
    push(B0_TOQ, stage.at[0])
    left = left.astype(BF16).reshape(t, t, hid)
    right = right.astype(BF16).reshape(t, t, hid)
    drop(A0_ROW, q, left)
    push(A0_ROW, buf.at[A0_ROW, q])
    gate0 = gate_of(0, normed0)
    hidden0 = product(A0_ROW, B0_TOQ, True, q)
    hidden0 = hidden0.astype(BF16).astype(F32)
    hid0, hid_inv0, update0, middle = finish(0, hidden0, x0, gate0)
    x1 = middle.astype(BF16).astype(F32)

    wait_weight(1)
    hat1, inv1, normed1, left1, right1 = enter(1, x1)
    left1 = left1.astype(BF16).reshape(t, t, hid)
    right1 = right1.astype(BF16).reshape(t, t, hid)
    drop(A1_ROW, q, left1)
    pl.when(same)(lambda: drop(A1_TOR, r, left1))
    push(A1_TOR, buf.at[A1_ROW, q])
    drop(B1_COL, r, right1)
    push(B1_COL, buf.at[B1_COL, r])
    push(A1_ROW, buf.at[A1_ROW, q])
    drop(B1_ROW, q, right1)
    push(B1_ROW, buf.at[B1_ROW, q])
    gate1 = gate_of(1, normed1)
    hidden1 = product(A1_TOR, B1_COL, False, r)
    hidden1 = hidden1.astype(BF16).astype(F32)
    hid1, hid_inv1, update1, final = finish(1, hidden1, x1, gate1)

    grad2 = cot_ref[...].astype(F32).reshape(cells, ch)
    d_hidden, d_logit = leave(1, grad2, gate1, update1, hid1, hid_inv1)
    turned1 = jnp.swapaxes(d_hidden.reshape(t, t, hid), 0, 1).astype(BF16)
    stage[1] = turned1
    pl.when(same)(lambda: drop(D1_TOQ, q, turned1))
    push(D1_TOQ, stage.at[1])
    drop(D1_COL, r, d_hidden.astype(BF16).reshape(t, t, hid))
    push(D1_COL, buf.at[D1_COL, r])
    new_ref[...] = final.astype(BF16).reshape(t, t, ch)
    drop(A0_COL, r, left)
    push(A0_COL, buf.at[A0_COL, r])
    drop(B0_COL, r, right)
    push(B0_COL, buf.at[B0_COL, r])
    d_normed = dot_t(d_logit.astype(BF16), gate_proj_ref[1])
    d_right = product(A1_ROW, D1_COL, True, r)
    d_left = product(B1_ROW, D1_TOQ, True, q)
    grad1 = entry(1, grad2, d_left, d_right, d_normed, hat1, inv1)

    d_hidden, d_logit = leave(0, grad1, gate0, update0, hid0, hid_inv0)
    d_hidden = d_hidden.astype(BF16).reshape(t, t, hid)
    drop(D0_ROW, q, d_hidden)
    pl.when(same)(lambda: drop(D0_TOR, r, d_hidden))
    push(D0_TOR, buf.at[D0_ROW, q])
    push(D0_ROW, buf.at[D0_ROW, q])
    d_normed = dot_t(d_logit.astype(BF16), gate_proj_ref[0])
    d_left = product(D0_ROW, B0_COL, True, q)
    d_right = product(D0_TOR, A0_COL, False, r)
    grad0 = entry(0, grad1, d_left, d_right, d_normed, hat0, inv0)
    grad_ref[...] = grad0.reshape(t, t, ch)

    for copy in weight_copies:
        copy.wait_send()
    for copy, maybe_self in pending:
        if maybe_self:
            pl.when(jnp.logical_not(same))(copy.wait_send)
        else:
            copy.wait_send()


def shards(
    n,
    n_chan,
    pair,
    window_start,
    residue_mask,
    in_gain,
    in_proj,
    gate_proj,
    out_gain,
    out_proj,
    cotangent,
):
    t, half, ch = cotangent.shape
    hid = out_proj.shape[1]
    turned = jnp.transpose(in_proj, (0, 2, 3, 1))
    vmem = pl.BlockSpec(memory_space=pltpu.VMEM)
    smem = pl.BlockSpec(memory_space=pltpu.SMEM)
    return pl.pallas_call(
        functools.partial(kernel, n, n_chan),
        out_shape=(
            jax.ShapeDtypeStruct((t, half, ch), BF16),
            jax.ShapeDtypeStruct((t, half, ch), F32),
        ),
        in_specs=[vmem, smem, smem] + [vmem] * 6,
        out_specs=(vmem, vmem),
        scratch_shapes=[
            pltpu.VMEM((KINDS, n, t, t, hid), BF16),
            pltpu.VMEM((2, t, t, hid), BF16),
            pltpu.VMEM((2, 4, hid, ch), BF16),
            pltpu.VMEM((t, t, ch), F32),
            pltpu.VMEM((t, t, hid), F32),
            pltpu.VMEM((t, t, hid), F32),
            pltpu.VMEM((2, t * t, 4 * hid), F32),
            pltpu.VMEM((t * t, 4 * hid), BF16),
            pltpu.SemaphoreType.DMA((KINDS, n)),
            pltpu.SemaphoreType.DMA((KINDS, n)),
            pltpu.SemaphoreType.DMA((2, n_chan)),
            pltpu.SemaphoreType.DMA((2, n_chan)),
        ],
        compiler_params=pltpu.CompilerParams(
            collective_id=0, has_side_effects=True, vmem_limit_bytes=40 * 1024 * 1024
        ),
    )(pair, window_start, residue_mask, in_gain, turned, gate_proj, out_gain, out_proj, cotangent)


def solution(mesh):
    n = mesh.shape["row"]
    n_chan = mesh.shape["chan"]
    assert n == mesh.shape["col"] * n_chan
    placed = (
        P(("grp", "row"), "col", None),
        P("grp"),
        P("grp"),
        P(),
        P(None, None, None, "chan"),
        P(),
        P(),
        P(),
        P(("grp", "row"), ("col", "chan"), None),
    )
    out = P(("grp", "row"), ("col", "chan"), None)
    return jax.shard_map(
        functools.partial(shards, n, n_chan),
        mesh=mesh,
        in_specs=placed,
        out_specs=(out, out),
        check_vma=False,
    )
```

```python
import functools

import jax
import jax.numpy as jnp
from jax import lax
from jax.experimental import pallas as pl
from jax.experimental.pallas import tpu as pltpu
from jax.sharding import PartitionSpec as P

F32 = jnp.float32
BF16 = jnp.bfloat16
MESH = pl.DeviceIdType.MESH

B0, A1, D1, D0, H0, H1, L1, R0 = range(8)
KINDS = 8
IN_ROW = (A1, D0, H0, L1)


def dot(a, b):
    return lax.dot_general(a, b, (((1,), (0,)), ((), ())), preferred_element_type=F32)


def dot_t(a, b):
    return lax.dot_general(a, b, (((1,), (1,)), ((), ())), preferred_element_type=F32)


def unit(x):
    center = x - jnp.mean(x, axis=-1, keepdims=True)
    inv = lax.rsqrt(jnp.mean(center * center, axis=-1, keepdims=True) + 1e-05)
    return center * inv, inv


def unit_back(hat, inv, d_hat):
    mean = jnp.mean(d_hat, axis=-1, keepdims=True)
    slope = jnp.mean(d_hat * hat, axis=-1, keepdims=True)
    return inv * (d_hat - mean - hat * slope)


def kernel(
    n,
    n_chan,
    pair_ref,
    start_ref,
    residue_ref,
    in_gain_ref,
    in_proj_ref,
    gate_proj_ref,
    out_gain_ref,
    out_proj_ref,
    cot_ref,
    new_ref,
    grad_ref,
    buf,
    stage,
    weight,
    mask_ref,
    lhs_ref,
    acc_ref,
    local,
    proj_ref,
    wide_ref,
    send_sem,
    recv_sem,
    weight_send,
    weight_recv,
):
    t = pair_ref.shape[0]
    ch = pair_ref.shape[2]
    hid = weight.shape[2]
    cells = t * t
    r = lax.axis_index("row")
    chan = lax.axis_index("chan")
    q = lax.axis_index("col") * n_chan + chan

    def peer(in_row, place):
        if in_row:
            return {"col": place // n_chan, "chan": lax.rem(place, n_chan)}
        return {"row": place}

    def here(kind):
        return q if kind in IN_ROW else r

    def after(place, d):
        return lax.rem(place + d, n)

    barrier = pltpu.get_barrier_semaphore()
    for in_row in (True, False):
        for d in range(1, n):
            pl.semaphore_signal(
                barrier,
                inc=1,
                device_id=peer(in_row, after(q if in_row else r, d)),
                device_id_type=MESH,
            )
    pl.semaphore_wait(barrier, 2 * (n - 1))

    def move(kind, place, source):
        return pltpu.make_async_remote_copy(
            src_ref=source,
            dst_ref=buf.at[kind, here(kind)],
            send_sem=send_sem.at[kind, place],
            recv_sem=recv_sem.at[kind, here(kind)],
            device_id=peer(kind in IN_ROW, place),
            device_id_type=MESH,
        )

    def share(kind, value):
        buf[kind, here(kind)] = value
        for d in range(1, n):
            move(kind, after(here(kind), d), buf.at[kind, here(kind)]).start()

    def arrive(kind, slot):
        copy = pltpu.make_async_remote_copy(
            src_ref=buf.at[kind, slot],
            dst_ref=buf.at[kind, slot],
            send_sem=send_sem.at[kind, slot],
            recv_sem=recv_sem.at[kind, slot],
            device_id=peer(kind in IN_ROW, slot),
            device_id_type=MESH,
        )
        pl.when(slot != here(kind))(copy.wait_recv)

    part = in_proj_ref.shape[2]
    mine = pl.ds(pl.multiple_of(chan * part, part), part)
    weight_copies = []
    for u in range(2):
        for d in range(1, n_chan):
            copy = pltpu.make_async_remote_copy(
                src_ref=in_proj_ref.at[u],
                dst_ref=weight.at[u, :, mine, :],
                send_sem=weight_send.at[u, d - 1],
                recv_sem=weight_recv.at[u, chan],
                device_id={"chan": lax.rem(chan + d, n_chan)},
                device_id_type=MESH,
            )
            copy.start()
            weight_copies.append(copy)
    weight[:, :, mine, :] = in_proj_ref[...]

    first = start_ref[0]
    rows = lax.broadcasted_iota(jnp.int32, (t, ch), 0)
    col_mask = jnp.zeros((t, ch), F32)
    for j in range(t):
        value = residue_ref[first + q * t + j].astype(F32)
        col_mask = jnp.where(rows == j, value, col_mask)
    for i in range(t):
        mask_ref[i] = col_mask * residue_ref[first + r * t + i].astype(F32)

    def wait_weight(u):
        for d in range(1, n_chan):
            other = lax.rem(chan + d, n_chan)
            theirs = pl.ds(pl.multiple_of(other * part, part), part)
            pltpu.make_async_remote_copy(
                src_ref=in_proj_ref.at[u],
                dst_ref=weight.at[u, :, theirs, :],
                send_sem=weight_send.at[u, d - 1],
                recv_sem=weight_recv.at[u, other],
                device_id={"chan": other},
                device_id_type=MESH,
            ).wait_recv()

    def enter(u, x):
        hat, inv = unit(x)
        normed = (hat * in_gain_ref[u : u + 1, :]).astype(BF16)
        wide = weight[u].reshape(4 * hid, ch)
        proj_ref[u] = dot_t(normed, wide)
        mask = mask_ref[...].reshape(cells, ch)
        left = jax.nn.sigmoid(proj_ref[u, :, 0:hid]) * proj_ref[u, :, hid : 2 * hid] * mask
        right = (
            jax.nn.sigmoid(proj_ref[u, :, 2 * hid : 3 * hid])
            * proj_ref[u, :, 3 * hid : 4 * hid]
            * mask
        )
        return hat, inv, normed, left, right

    def gate_of(u, normed):
        return jax.nn.sigmoid(dot(normed, gate_proj_ref[u]))

    def multiply(left_major, right_of):
        for low in range(0, t, 8):
            acc = acc_ref[low : low + 8]
            for k in range(t):
                if left_major:
                    left = lhs_ref[low : low + 8, k : k + 1, :]
                else:
                    left = lhs_ref[k, low : low + 8, :].reshape(8, 1, hid)
                acc = acc + left * right_of(k)[None]
            acc_ref[low : low + 8] = acc

    def product(left_kind, right_kind):
        acc_ref[...] = jnp.zeros_like(acc_ref)

        def body(s, carry):
            lhs_ref[...] = buf[left_kind, s].astype(F32)
            multiply(True, lambda k: buf[right_kind, s, k].astype(F32))
            return carry

        lax.fori_loop(0, n, body, 0)
        return acc_ref[...].reshape(cells, hid)

    def partials(kind, out_kind, left_major):
        def body(d, carry):
            s = after(here(kind), n - d)
            arrive(kind, s)
            lhs_ref[...] = buf[kind, s].astype(F32)
            acc_ref[...] = jnp.zeros_like(acc_ref)
            multiply(left_major, lambda k: local[k])
            out = stage.at[out_kind - H0, s]
            out[...] = acc_ref[...].astype(BF16)

            @pl.when(s != here(out_kind))
            def _():
                move(out_kind, s, out).start()

            @pl.when(s == here(out_kind))
            def _():
                buf[out_kind, s] = acc_ref[...].astype(BF16)

            return carry

        lax.fori_loop(0, n, body, 0)

    def total(kind):
        acc_ref[...] = jnp.zeros_like(acc_ref)

        def body(d, carry):
            s = after(here(kind), n - d)
            arrive(kind, s)
            acc_ref[...] += buf[kind, s].astype(F32)
            return carry

        lax.fori_loop(0, n, body, 0)
        return acc_ref[...]

    def turn(value):
        return jnp.swapaxes(value.reshape(t, t, hid), 0, 1)

    def finish(u, hidden, x, gate):
        hat, inv = unit(hidden)
        scaled = (hat * out_gain_ref[u : u + 1, :]).astype(BF16)
        update = dot(scaled, out_proj_ref[u])
        return hat, inv, update, x + gate * update

    def leave(u, grad, gate, update, hat, inv):
        d_update = grad * gate
        d_logit = d_update * update * (1.0 - gate)
        d_scaled = dot_t(d_update.astype(BF16), out_proj_ref[u])
        d_hidden = unit_back(hat, inv, d_scaled * out_gain_ref[u : u + 1, :])
        return d_hidden, d_logit

    def entry(u, grad, d_left, d_right, d_normed, hat, inv):
        mask = mask_ref[...].reshape(cells, ch)
        for side, value in ((0, d_left * mask), (2, d_right * mask)):
            gate = jax.nn.sigmoid(proj_ref[u, :, side * hid : (side + 1) * hid])
            held = proj_ref[u, :, (side + 1) * hid : (side + 2) * hid]
            slope = value * gate
            wide_ref[:, side * hid : (side + 1) * hid] = (slope * held * (1.0 - gate)).astype(BF16)
            wide_ref[:, (side + 1) * hid : (side + 2) * hid] = slope.astype(BF16)
        d_entry = dot(wide_ref[...], weight[u].reshape(4 * hid, ch))
        return grad + unit_back(hat, inv, (d_entry + d_normed) * in_gain_ref[u : u + 1, :])

    own = pl.ds(pl.multiple_of(chan * t, t), t)
    x0 = pair_ref[:, own, :].astype(F32).reshape(cells, ch)
    wait_weight(0)
    hat0, inv0, normed0, left, right = enter(0, x0)
    share(B0, right.astype(BF16).reshape(t, t, hid))
    left0 = left.astype(BF16).astype(F32).reshape(t, t, hid)
    local[...] = turn(left0)
    gate0 = gate_of(0, normed0)
    partials(B0, H0, True)
    hidden0 = turn(total(H0)).reshape(cells, hid).astype(BF16).astype(F32)
    hid0, hid_inv0, update0, middle = finish(0, hidden0, x0, gate0)
    x1 = middle.astype(BF16).astype(F32)

    wait_weight(1)
    hat1, inv1, normed1, left, right = enter(1, x1)
    share(A1, left.astype(BF16).reshape(t, t, hid))
    right1 = right.astype(BF16).astype(F32).reshape(t, t, hid)
    local[...] = right1
    gate1 = gate_of(1, normed1)
    partials(A1, H1, False)
    local[...] = turn(right1)
    hidden1 = total(H1).reshape(cells, hid).astype(BF16).astype(F32)
    hid1, hid_inv1, update1, final = finish(1, hidden1, x1, gate1)

    grad2 = cot_ref[...].astype(F32).reshape(cells, ch)
    d_hidden, d_logit = leave(1, grad2, gate1, update1, hid1, hid_inv1)
    share(D1, d_hidden.astype(BF16).reshape(t, t, hid))
    new_ref[...] = final.astype(BF16).reshape(t, t, ch)
    d_normed = dot_t(d_logit.astype(BF16), gate_proj_ref[1])
    partials(D1, L1, True)
    d_right = product(A1, D1)
    d_left = turn(total(L1)).reshape(cells, hid)
    grad1 = entry(1, grad2, d_left, d_right, d_normed, hat1, inv1)

    d_hidden, d_logit = leave(0, grad1, gate0, update0, hid0, hid_inv0)
    share(D0, d_hidden.astype(BF16).reshape(t, t, hid))
    local[...] = left0
    d_normed = dot_t(d_logit.astype(BF16), gate_proj_ref[0])
    partials(D0, R0, False)
    d_left = product(D0, B0)
    d_right = total(R0).reshape(cells, hid)
    grad0 = entry(0, grad1, d_left, d_right, d_normed, hat0, inv0)
    grad_ref[...] = grad0.reshape(t, t, ch)

    for copy in weight_copies:
        copy.wait_send()
    for kind in range(KINDS):
        for d in range(1, n):
            move(kind, after(here(kind), d), buf.at[kind, here(kind)]).wait_send()


def shards(
    n,
    n_chan,
    pair,
    window_start,
    residue_mask,
    in_gain,
    in_proj,
    gate_proj,
    out_gain,
    out_proj,
    cotangent,
):
    t, half, ch = cotangent.shape
    hid = out_proj.shape[1]
    turned = jnp.transpose(in_proj, (0, 2, 3, 1))
    vmem = pl.BlockSpec(memory_space=pltpu.VMEM)
    smem = pl.BlockSpec(memory_space=pltpu.SMEM)
    return pl.pallas_call(
        functools.partial(kernel, n, n_chan),
        out_shape=(
            jax.ShapeDtypeStruct((t, half, ch), BF16),
            jax.ShapeDtypeStruct((t, half, ch), F32),
        ),
        in_specs=[vmem, smem, smem] + [vmem] * 6,
        out_specs=(vmem, vmem),
        scratch_shapes=[
            pltpu.VMEM((KINDS, n, t, t, hid), BF16),
            pltpu.VMEM((KINDS - H0, n, t, t, hid), BF16),
            pltpu.VMEM((2, 4, hid, ch), BF16),
            pltpu.VMEM((t, t, ch), F32),
            pltpu.VMEM((t, t, hid), F32),
            pltpu.VMEM((t, t, hid), F32),
            pltpu.VMEM((t, t, hid), F32),
            pltpu.VMEM((2, t * t, 4 * hid), F32),
            pltpu.VMEM((t * t, 4 * hid), BF16),
            pltpu.SemaphoreType.DMA((KINDS, n)),
            pltpu.SemaphoreType.DMA((KINDS, n)),
            pltpu.SemaphoreType.DMA((2, n_chan)),
            pltpu.SemaphoreType.DMA((2, n_chan)),
        ],
        compiler_params=pltpu.CompilerParams(
            collective_id=0, has_side_effects=True, vmem_limit_bytes=40 * 1024 * 1024
        ),
    )(pair, window_start, residue_mask, in_gain, turned, gate_proj, out_gain, out_proj, cotangent)


def solution(mesh):
    n = mesh.shape["row"]
    n_chan = mesh.shape["chan"]
    assert n == mesh.shape["col"] * n_chan
    placed = (
        P(("grp", "row"), "col", None),
        P("grp"),
        P("grp"),
        P(),
        P(None, None, None, "chan"),
        P(),
        P(),
        P(),
        P(("grp", "row"), ("col", "chan"), None),
    )
    out = P(("grp", "row"), ("col", "chan"), None)
    return jax.shard_map(
        functools.partial(shards, n, n_chan),
        mesh=mesh,
        in_specs=placed,
        out_specs=(out, out),
        check_vma=False,
    )
```

```python
import functools

import jax
import jax.numpy as jnp
from jax import lax
from jax.experimental import pallas as pl
from jax.experimental.pallas import tpu as pltpu
from jax.sharding import PartitionSpec as P

F32 = jnp.float32
BF16 = jnp.bfloat16
MESH = pl.DeviceIdType.MESH

B0, A1, D1, D0, H0, H1, L1, R0 = range(8)
KINDS = 8
IN_ROW = (A1, D0, H0, L1)


def dot(a, b):
    return lax.dot_general(a, b, (((1,), (0,)), ((), ())), preferred_element_type=F32)


def dot_t(a, b):
    return lax.dot_general(a, b, (((1,), (1,)), ((), ())), preferred_element_type=F32)


def unit(x):
    center = x - jnp.mean(x, axis=-1, keepdims=True)
    inv = lax.rsqrt(jnp.mean(center * center, axis=-1, keepdims=True) + 1e-05)
    return center * inv, inv


def unit_back(hat, inv, d_hat):
    mean = jnp.mean(d_hat, axis=-1, keepdims=True)
    slope = jnp.mean(d_hat * hat, axis=-1, keepdims=True)
    return inv * (d_hat - mean - hat * slope)


def kernel(
    n,
    n_chan,
    pair_hbm,
    start_ref,
    residue_hbm,
    in_gain_hbm,
    in_proj_ref,
    gate_proj_hbm,
    out_gain_hbm,
    out_proj_hbm,
    cot_hbm,
    new_hbm,
    grad_hbm,
    new_ref,
    grad_ref,
    pair_ref,
    residue_ref,
    in_gain_ref,
    gate_proj_ref,
    out_gain_ref,
    out_proj_ref,
    cot_ref,
    load_sem,
    out_sem,
    buf,
    stage,
    weight,
    mask_ref,
    lhs_ref,
    acc_ref,
    local,
    proj_ref,
    wide_ref,
    send_sem,
    recv_sem,
    weight_send,
    weight_recv,
):
    t = cot_ref.shape[0]
    ch = cot_ref.shape[2]
    hid = weight.shape[2]
    cells = t * t
    r = lax.axis_index("row")
    chan = lax.axis_index("chan")
    q = lax.axis_index("col") * n_chan + chan

    def peer(in_row, place):
        if in_row:
            return {"col": place // n_chan, "chan": lax.rem(place, n_chan)}
        return {"row": place}

    def here(kind):
        return q if kind in IN_ROW else r

    def after(place, d):
        return lax.rem(place + d, n)

    part = in_proj_ref.shape[2]
    mine = pl.ds(pl.multiple_of(chan * part, part), part)
    own = pl.ds(pl.multiple_of(chan * t, t), t)
    loads = [
        pltpu.make_async_copy(source, target, load_sem.at[place])
        for place, (source, target) in enumerate(
            (
                (pair_hbm.at[:, own, :], pair_ref),
                (in_proj_ref, weight.at[:, :, mine, :]),
                (in_gain_hbm, in_gain_ref),
                (residue_hbm, residue_ref),
                (gate_proj_hbm, gate_proj_ref),
                (out_gain_hbm, out_gain_ref),
                (out_proj_hbm, out_proj_ref),
                (cot_hbm, cot_ref),
            )
        )
    ]
    for load in loads:
        load.start()

    barrier = pltpu.get_barrier_semaphore()
    for in_row in (True, False):
        for d in range(1, n):
            pl.semaphore_signal(
                barrier,
                inc=1,
                device_id=peer(in_row, after(q if in_row else r, d)),
                device_id_type=MESH,
            )
    pl.semaphore_wait(barrier, 2 * (n - 1))

    def move(kind, place, source):
        return pltpu.make_async_remote_copy(
            src_ref=source,
            dst_ref=buf.at[kind, here(kind)],
            send_sem=send_sem.at[kind, place],
            recv_sem=recv_sem.at[kind, here(kind)],
            device_id=peer(kind in IN_ROW, place),
            device_id_type=MESH,
        )

    def share(kind, value):
        buf[kind, here(kind)] = value
        for d in range(1, n):
            move(kind, after(here(kind), d), buf.at[kind, here(kind)]).start()

    def arrive(kind, slot):
        copy = pltpu.make_async_remote_copy(
            src_ref=buf.at[kind, slot],
            dst_ref=buf.at[kind, slot],
            send_sem=send_sem.at[kind, slot],
            recv_sem=recv_sem.at[kind, slot],
            device_id=peer(kind in IN_ROW, slot),
            device_id_type=MESH,
        )
        pl.when(slot != here(kind))(copy.wait_recv)

    weight_copies = []
    for u in range(2):
        for d in range(1, n_chan):
            copy = pltpu.make_async_remote_copy(
                src_ref=in_proj_ref.at[u],
                dst_ref=weight.at[u, :, mine, :],
                send_sem=weight_send.at[u, d - 1],
                recv_sem=weight_recv.at[u, chan],
                device_id={"chan": lax.rem(chan + d, n_chan)},
                device_id_type=MESH,
            )
            copy.start()
            weight_copies.append(copy)
    for load in loads:
        load.wait()

    first = start_ref[0]
    rows = lax.broadcasted_iota(jnp.int32, (t, ch), 0)
    col_mask = jnp.zeros((t, ch), F32)
    for j in range(t):
        value = residue_ref[first + q * t + j].astype(F32)
        col_mask = jnp.where(rows == j, value, col_mask)
    for i in range(t):
        mask_ref[i] = col_mask * residue_ref[first + r * t + i].astype(F32)

    def wait_weight(u):
        for d in range(1, n_chan):
            other = lax.rem(chan + d, n_chan)
            theirs = pl.ds(pl.multiple_of(other * part, part), part)
            pltpu.make_async_remote_copy(
                src_ref=in_proj_ref.at[u],
                dst_ref=weight.at[u, :, theirs, :],
                send_sem=weight_send.at[u, d - 1],
                recv_sem=weight_recv.at[u, other],
                device_id={"chan": other},
                device_id_type=MESH,
            ).wait_recv()

    def enter(u, x):
        hat, inv = unit(x)
        return hat, inv, (hat * in_gain_ref[u : u + 1, :]).astype(BF16)

    def gated(u, normed, side):
        low, middle, high = side * hid, (side + 1) * hid, (side + 2) * hid
        wide = weight[u, side : side + 2].reshape(2 * hid, ch)
        proj_ref[u, :, low:high] = dot_t(normed, wide)
        mask = mask_ref[...].reshape(cells, ch)
        value = jax.nn.sigmoid(proj_ref[u, :, low:middle]) * proj_ref[u, :, middle:high] * mask
        return value.astype(BF16).reshape(t, t, hid)

    def gate_of(u, normed):
        return jax.nn.sigmoid(dot(normed, gate_proj_ref[u]))

    def multiply(left_major, right_of):
        for low in range(0, t, 8):
            acc = acc_ref[low : low + 8]
            for k in range(t):
                if left_major:
                    left = lhs_ref[low : low + 8, k : k + 1, :]
                else:
                    left = lhs_ref[k, low : low + 8, :].reshape(8, 1, hid)
                acc = acc + left * right_of(k)[None]
            acc_ref[low : low + 8] = acc

    def product(left_kind, right_kind):
        acc_ref[...] = jnp.zeros_like(acc_ref)

        def body(s, carry):
            lhs_ref[...] = buf[left_kind, s].astype(F32)
            multiply(True, lambda k: buf[right_kind, s, k].astype(F32))
            return carry

        lax.fori_loop(0, n, body, 0)
        return acc_ref[...].reshape(cells, hid)

    def partials(kind, out_kind, left_major):
        def body(d, carry):
            s = after(here(kind), n - d)
            arrive(kind, s)
            lhs_ref[...] = buf[kind, s].astype(F32)
            acc_ref[...] = jnp.zeros_like(acc_ref)
            multiply(left_major, lambda k: local[k])
            out = stage.at[out_kind - H0, s]
            out[...] = acc_ref[...].astype(BF16)

            @pl.when(s != here(out_kind))
            def _():
                move(out_kind, s, out).start()

            @pl.when(s == here(out_kind))
            def _():
                buf[out_kind, s] = acc_ref[...].astype(BF16)

            return carry

        lax.fori_loop(0, n, body, 0)

    def total(kind):
        acc_ref[...] = jnp.zeros_like(acc_ref)

        def body(d, carry):
            s = after(here(kind), n - d)
            arrive(kind, s)
            acc_ref[...] += buf[kind, s].astype(F32)
            return carry

        lax.fori_loop(0, n, body, 0)
        return acc_ref[...]

    def turn(value):
        return jnp.swapaxes(value.reshape(t, t, hid), 0, 1)

    def finish(u, hidden, x, gate):
        hat, inv = unit(hidden)
        scaled = (hat * out_gain_ref[u : u + 1, :]).astype(BF16)
        update = dot(scaled, out_proj_ref[u])
        return hat, inv, update, x + gate * update

    def leave(u, grad, gate, update, hat, inv):
        d_update = grad * gate
        d_logit = d_update * update * (1.0 - gate)
        d_scaled = dot_t(d_update.astype(BF16), out_proj_ref[u])
        d_hidden = unit_back(hat, inv, d_scaled * out_gain_ref[u : u + 1, :])
        return d_hidden, d_logit

    def entry(u, grad, d_left, d_right, d_normed, hat, inv):
        mask = mask_ref[...].reshape(cells, ch)
        for side, value in ((0, d_left * mask), (2, d_right * mask)):
            gate = jax.nn.sigmoid(proj_ref[u, :, side * hid : (side + 1) * hid])
            held = proj_ref[u, :, (side + 1) * hid : (side + 2) * hid]
            slope = value * gate
            wide_ref[:, side * hid : (side + 1) * hid] = (slope * held * (1.0 - gate)).astype(BF16)
            wide_ref[:, (side + 1) * hid : (side + 2) * hid] = slope.astype(BF16)
        d_entry = dot(wide_ref[...], weight[u].reshape(4 * hid, ch))
        return grad + unit_back(hat, inv, (d_entry + d_normed) * in_gain_ref[u : u + 1, :])

    x0 = pair_ref[...].astype(F32).reshape(cells, ch)
    hat0, inv0, normed0 = enter(0, x0)
    wait_weight(0)
    share(B0, gated(0, normed0, 2))
    left0 = gated(0, normed0, 0).astype(F32)
    local[...] = turn(left0)
    gate0 = gate_of(0, normed0)
    partials(B0, H0, True)
    hidden0 = turn(total(H0)).reshape(cells, hid).astype(BF16).astype(F32)
    hid0, hid_inv0, update0, middle = finish(0, hidden0, x0, gate0)
    x1 = middle.astype(BF16).astype(F32)

    hat1, inv1, normed1 = enter(1, x1)
    wait_weight(1)
    share(A1, gated(1, normed1, 0))
    right1 = gated(1, normed1, 2).astype(F32)
    local[...] = right1
    gate1 = gate_of(1, normed1)
    partials(A1, H1, False)
    local[...] = turn(right1)
    hidden1 = total(H1).reshape(cells, hid).astype(BF16).astype(F32)
    hid1, hid_inv1, update1, final = finish(1, hidden1, x1, gate1)

    grad2 = cot_ref[...].astype(F32).reshape(cells, ch)
    d_hidden, d_logit = leave(1, grad2, gate1, update1, hid1, hid_inv1)
    share(D1, d_hidden.astype(BF16).reshape(t, t, hid))
    new_ref[...] = final.astype(BF16).reshape(t, t, ch)
    new_out = pltpu.make_async_copy(new_ref, new_hbm, out_sem.at[0])
    new_out.start()
    d_normed = dot_t(d_logit.astype(BF16), gate_proj_ref[1])
    partials(D1, L1, True)
    d_right = product(A1, D1)
    d_left = turn(total(L1)).reshape(cells, hid)
    grad1 = entry(1, grad2, d_left, d_right, d_normed, hat1, inv1)

    d_hidden, d_logit = leave(0, grad1, gate0, update0, hid0, hid_inv0)
    share(D0, d_hidden.astype(BF16).reshape(t, t, hid))
    local[...] = left0
    d_normed = dot_t(d_logit.astype(BF16), gate_proj_ref[0])
    partials(D0, R0, False)
    d_left = product(D0, B0)
    d_right = total(R0).reshape(cells, hid)
    grad0 = entry(0, grad1, d_left, d_right, d_normed, hat0, inv0)
    grad_ref[...] = grad0.reshape(t, t, ch)
    grad_out = pltpu.make_async_copy(grad_ref, grad_hbm, out_sem.at[1])
    grad_out.start()

    for copy in weight_copies:
        copy.wait_send()
    new_out.wait()
    for kind in range(KINDS):
        for d in range(1, n):
            move(kind, after(here(kind), d), buf.at[kind, here(kind)]).wait_send()
    grad_out.wait()


def shards(
    n,
    n_chan,
    pair,
    window_start,
    residue_mask,
    in_gain,
    in_proj,
    gate_proj,
    out_gain,
    out_proj,
    cotangent,
):
    t, half, ch = cotangent.shape
    hid = out_proj.shape[1]
    turned = jnp.transpose(in_proj, (0, 2, 3, 1))
    hbm = pl.BlockSpec(memory_space=pltpu.HBM)
    smem = pl.BlockSpec(memory_space=pltpu.SMEM)
    return pl.pallas_call(
        functools.partial(kernel, n, n_chan),
        out_shape=(
            jax.ShapeDtypeStruct((t, half, ch), BF16),
            jax.ShapeDtypeStruct((t, half, ch), F32),
        ),
        in_specs=[hbm, smem] + [hbm] * 7,
        out_specs=(hbm, hbm),
        scratch_shapes=[
            pltpu.VMEM((t, half, ch), BF16),
            pltpu.VMEM((t, half, ch), F32),
            pltpu.VMEM((t, half, ch), BF16),
            pltpu.SMEM(residue_mask.shape, jnp.int32),
            pltpu.VMEM(in_gain.shape, F32),
            pltpu.VMEM(gate_proj.shape, BF16),
            pltpu.VMEM(out_gain.shape, F32),
            pltpu.VMEM(out_proj.shape, BF16),
            pltpu.VMEM((t, half, ch), BF16),
            pltpu.SemaphoreType.DMA((8,)),
            pltpu.SemaphoreType.DMA((2,)),
            pltpu.VMEM((KINDS, n, t, t, hid), BF16),
            pltpu.VMEM((KINDS - H0, n, t, t, hid), BF16),
            pltpu.VMEM((2, 4, hid, ch), BF16),
            pltpu.VMEM((t, t, ch), F32),
            pltpu.VMEM((t, t, hid), F32),
            pltpu.VMEM((t, t, hid), F32),
            pltpu.VMEM((t, t, hid), F32),
            pltpu.VMEM((2, t * t, 4 * hid), F32),
            pltpu.VMEM((t * t, 4 * hid), BF16),
            pltpu.SemaphoreType.DMA((KINDS, n)),
            pltpu.SemaphoreType.DMA((KINDS, n)),
            pltpu.SemaphoreType.DMA((2, n_chan)),
            pltpu.SemaphoreType.DMA((2, n_chan)),
        ],
        compiler_params=pltpu.CompilerParams(
            collective_id=0, has_side_effects=True, vmem_limit_bytes=64 * 1024 * 1024
        ),
    )(pair, window_start, residue_mask, in_gain, turned, gate_proj, out_gain, out_proj, cotangent)


def solution(mesh):
    n = mesh.shape["row"]
    n_chan = mesh.shape["chan"]
    assert n == mesh.shape["col"] * n_chan
    placed = (
        P(("grp", "row"), "col", None),
        P("grp"),
        P("grp"),
        P(),
        P(None, None, None, "chan"),
        P(),
        P(),
        P(),
        P(("grp", "row"), ("col", "chan"), None),
    )
    out = P(("grp", "row"), ("col", "chan"), None)
    return jax.shard_map(
        functools.partial(shards, n, n_chan),
        mesh=mesh,
        in_specs=placed,
        out_specs=(out, out),
        check_vma=False,
    )
```

```python
import functools

import jax
import jax.numpy as jnp
from jax import lax
from jax.experimental import pallas as pl
from jax.experimental.pallas import tpu as pltpu
from jax.sharding import PartitionSpec as P

F32 = jnp.float32
BF16 = jnp.bfloat16
MESH = pl.DeviceIdType.MESH

B0, A1, D1, D0, H0, H1, L1, R0, PAIR = range(9)
KINDS = 9
IN_ROW = (A1, D0, H0, L1)


def dot(a, b):
    return lax.dot_general(a, b, (((1,), (0,)), ((), ())), preferred_element_type=F32)


def dot_t(a, b):
    return lax.dot_general(a, b, (((1,), (1,)), ((), ())), preferred_element_type=F32)


def unit(x):
    center = x - jnp.mean(x, axis=-1, keepdims=True)
    inv = lax.rsqrt(jnp.mean(center * center, axis=-1, keepdims=True) + 1e-05)
    return center * inv, inv


def unit_back(hat, inv, d_hat):
    mean = jnp.mean(d_hat, axis=-1, keepdims=True)
    slope = jnp.mean(d_hat * hat, axis=-1, keepdims=True)
    return inv * (d_hat - mean - hat * slope)


def kernel(
    n,
    n_chan,
    pair_hbm,
    start_ref,
    residue_hbm,
    in_gain_hbm,
    in_proj_ref,
    gate_proj_hbm,
    out_gain_hbm,
    out_proj_hbm,
    cot_hbm,
    new_hbm,
    grad_hbm,
    new_ref,
    grad_ref,
    pair_ref,
    residue_ref,
    in_gain_ref,
    gate_proj_ref,
    out_gain_ref,
    out_proj_ref,
    cot_ref,
    load_sem,
    out_sem,
    buf,
    stage,
    weight,
    mask_ref,
    mask_other,
    lhs_ref,
    acc_ref,
    local,
    proj_ref,
    wide_ref,
    send_sem,
    recv_sem,
    weight_send,
    weight_recv,
):
    t = cot_ref.shape[0]
    ch = cot_ref.shape[2]
    hid = weight.shape[2]
    cells = t * t
    r = lax.axis_index("row")
    chan = lax.axis_index("chan")
    q = lax.axis_index("col") * n_chan + chan

    def peer(in_row, place):
        if in_row:
            return {"col": place // n_chan, "chan": lax.rem(place, n_chan)}
        return {"row": place}

    def here(kind):
        return q if kind in IN_ROW else r

    def after(place, d):
        return lax.rem(place + d, n)

    part = in_proj_ref.shape[2]
    mine = pl.ds(pl.multiple_of(chan * part, part), part)
    own = pl.ds(pl.multiple_of(chan * t, t), t)
    loads = [
        pltpu.make_async_copy(source, target, load_sem.at[place])
        for place, (source, target) in enumerate(
            (
                (pair_hbm.at[:, own, :], pair_ref),
                (in_proj_ref, weight.at[:, :, mine, :]),
                (in_gain_hbm, in_gain_ref),
                (residue_hbm, residue_ref),
                (gate_proj_hbm, gate_proj_ref),
                (out_gain_hbm, out_gain_ref),
                (out_proj_hbm, out_proj_ref),
                (cot_hbm, cot_ref),
            )
        )
    ]
    for load in loads:
        load.start()

    barrier = pltpu.get_barrier_semaphore()
    for in_row in (True, False):
        for d in range(1, n):
            pl.semaphore_signal(
                barrier,
                inc=1,
                device_id=peer(in_row, after(q if in_row else r, d)),
                device_id_type=MESH,
            )
    pl.semaphore_wait(barrier, 2 * (n - 1))

    def move(kind, place, source):
        return pltpu.make_async_remote_copy(
            src_ref=source,
            dst_ref=buf.at[kind, here(kind)],
            send_sem=send_sem.at[kind, place],
            recv_sem=recv_sem.at[kind, here(kind)],
            device_id=peer(kind in IN_ROW, place),
            device_id_type=MESH,
        )

    def share(kind, value):
        buf[kind, here(kind)] = value
        for d in range(1, n):
            move(kind, after(here(kind), d), buf.at[kind, here(kind)]).start()

    def arrive(kind, slot):
        copy = pltpu.make_async_remote_copy(
            src_ref=buf.at[kind, slot],
            dst_ref=buf.at[kind, slot],
            send_sem=send_sem.at[kind, slot],
            recv_sem=recv_sem.at[kind, slot],
            device_id=peer(kind in IN_ROW, slot),
            device_id_type=MESH,
        )
        pl.when(slot != here(kind))(copy.wait_recv)

    loads[1].wait()
    weight_copies = []
    for u in range(2):
        for d in range(1, n_chan):
            copy = pltpu.make_async_remote_copy(
                src_ref=weight.at[u, :, mine, :],
                dst_ref=weight.at[u, :, mine, :],
                send_sem=weight_send.at[u, d - 1],
                recv_sem=weight_recv.at[u, chan],
                device_id={"chan": lax.rem(chan + d, n_chan)},
                device_id_type=MESH,
            )
            copy.start()
            weight_copies.append(copy)
    loads[0].wait()
    for d in range(1, n):
        move(PAIR, after(r, d), pair_ref).start()
    for load in loads[2:]:
        load.wait()

    first = start_ref[0]
    rows = lax.broadcasted_iota(jnp.int32, (t, ch), 0)
    col_mask = jnp.zeros((t, ch), F32)
    for j in range(t):
        value = residue_ref[first + q * t + j].astype(F32)
        col_mask = jnp.where(rows == j, value, col_mask)
    for i in range(t):
        mask_ref[i] = col_mask * residue_ref[first + r * t + i].astype(F32)

    def wait_weight(u):
        for d in range(1, n_chan):
            other = lax.rem(chan + d, n_chan)
            theirs = pl.ds(pl.multiple_of(other * part, part), part)
            pltpu.make_async_remote_copy(
                src_ref=weight.at[u, :, theirs, :],
                dst_ref=weight.at[u, :, theirs, :],
                send_sem=weight_send.at[u, d - 1],
                recv_sem=weight_recv.at[u, other],
                device_id={"chan": other},
                device_id_type=MESH,
            ).wait_recv()

    def enter(u, x):
        hat, inv = unit(x)
        return hat, inv, (hat * in_gain_ref[u : u + 1, :]).astype(BF16)

    def gated(u, normed, side):
        low, middle, high = side * hid, (side + 1) * hid, (side + 2) * hid
        wide = weight[u, side : side + 2].reshape(2 * hid, ch)
        proj_ref[u, :, low:high] = dot_t(normed, wide)
        mask = mask_ref[...].reshape(cells, ch)
        value = jax.nn.sigmoid(proj_ref[u, :, low:middle]) * proj_ref[u, :, middle:high] * mask
        return value.astype(BF16).reshape(t, t, hid)

    def project_other(kind, s):
        @pl.when(s != r)
        def _():
            arrive(PAIR, s)
            normed = enter(0, buf[PAIR, s].astype(F32).reshape(cells, ch))[2]
            both = dot_t(normed, weight[0, 2:4].reshape(2 * hid, ch))
            for i in range(t):
                mask_other[i] = col_mask * residue_ref[first + s * t + i].astype(F32)
            mask = mask_other[...].reshape(cells, ch)
            value = jax.nn.sigmoid(both[:, :hid]) * both[:, hid:] * mask
            buf[kind, s] = value.astype(BF16).reshape(t, t, hid)

    def gate_of(u, normed):
        return jax.nn.sigmoid(dot(normed, gate_proj_ref[u]))

    def multiply(left_major, right_of):
        for low in range(0, t, 8):
            acc = acc_ref[low : low + 8]
            for k in range(t):
                if left_major:
                    left = lhs_ref[low : low + 8, k : k + 1, :]
                else:
                    left = lhs_ref[k, low : low + 8, :].reshape(8, 1, hid)
                acc = acc + left * right_of(k)[None]
            acc_ref[low : low + 8] = acc

    def product(left_kind, right_kind):
        acc_ref[...] = jnp.zeros_like(acc_ref)

        def body(s, carry):
            lhs_ref[...] = buf[left_kind, s].astype(F32)
            multiply(True, lambda k: buf[right_kind, s, k].astype(F32))
            return carry

        lax.fori_loop(0, n, body, 0)
        return acc_ref[...].reshape(cells, hid)

    def partials(kind, out_kind, left_major, fetch):
        def body(d, carry):
            s = after(here(kind), n - d)
            fetch(kind, s)
            lhs_ref[...] = buf[kind, s].astype(F32)
            acc_ref[...] = jnp.zeros_like(acc_ref)
            multiply(left_major, lambda k: local[k])
            out = stage.at[out_kind - H0, s]
            out[...] = acc_ref[...].astype(BF16)

            @pl.when(s != here(out_kind))
            def _():
                move(out_kind, s, out).start()

            @pl.when(s == here(out_kind))
            def _():
                buf[out_kind, s] = acc_ref[...].astype(BF16)

            return carry

        lax.fori_loop(0, n, body, 0)

    def total(kind):
        acc_ref[...] = jnp.zeros_like(acc_ref)

        def body(d, carry):
            s = after(here(kind), n - d)
            arrive(kind, s)
            acc_ref[...] += buf[kind, s].astype(F32)
            return carry

        lax.fori_loop(0, n, body, 0)
        return acc_ref[...]

    def turn(value):
        return jnp.swapaxes(value.reshape(t, t, hid), 0, 1)

    def finish(u, hidden, x, gate):
        hat, inv = unit(hidden)
        scaled = (hat * out_gain_ref[u : u + 1, :]).astype(BF16)
        update = dot(scaled, out_proj_ref[u])
        return hat, inv, update, x + gate * update

    def leave(u, grad, gate, update, hat, inv):
        d_update = grad * gate
        d_logit = d_update * update * (1.0 - gate)
        d_scaled = dot_t(d_update.astype(BF16), out_proj_ref[u])
        d_hidden = unit_back(hat, inv, d_scaled * out_gain_ref[u : u + 1, :])
        return d_hidden, d_logit

    def entry(u, grad, d_left, d_right, d_normed, hat, inv):
        mask = mask_ref[...].reshape(cells, ch)
        for side, value in ((0, d_left * mask), (2, d_right * mask)):
            gate = jax.nn.sigmoid(proj_ref[u, :, side * hid : (side + 1) * hid])
            held = proj_ref[u, :, (side + 1) * hid : (side + 2) * hid]
            slope = value * gate
            wide_ref[:, side * hid : (side + 1) * hid] = (slope * held * (1.0 - gate)).astype(BF16)
            wide_ref[:, (side + 1) * hid : (side + 2) * hid] = slope.astype(BF16)
        d_entry = dot(wide_ref[...], weight[u].reshape(4 * hid, ch))
        return grad + unit_back(hat, inv, (d_entry + d_normed) * in_gain_ref[u : u + 1, :])

    x0 = pair_ref[...].astype(F32).reshape(cells, ch)
    hat0, inv0, normed0 = enter(0, x0)
    wait_weight(0)
    buf[B0, r] = gated(0, normed0, 2)
    left0 = gated(0, normed0, 0).astype(F32)
    local[...] = turn(left0)
    partials(B0, H0, True, project_other)
    gate0 = gate_of(0, normed0)
    hidden0 = turn(total(H0)).reshape(cells, hid).astype(BF16).astype(F32)
    hid0, hid_inv0, update0, middle = finish(0, hidden0, x0, gate0)
    x1 = middle.astype(BF16).astype(F32)

    hat1, inv1, normed1 = enter(1, x1)
    wait_weight(1)
    share(A1, gated(1, normed1, 0))
    right1 = gated(1, normed1, 2).astype(F32)
    local[...] = right1
    partials(A1, H1, False, arrive)
    gate1 = gate_of(1, normed1)
    local[...] = turn(right1)
    hidden1 = total(H1).reshape(cells, hid).astype(BF16).astype(F32)
    hid1, hid_inv1, update1, final = finish(1, hidden1, x1, gate1)

    grad2 = cot_ref[...].astype(F32).reshape(cells, ch)
    d_hidden, d_logit = leave(1, grad2, gate1, update1, hid1, hid_inv1)
    share(D1, d_hidden.astype(BF16).reshape(t, t, hid))
    partials(D1, L1, True, arrive)
    new_ref[...] = final.astype(BF16).reshape(t, t, ch)
    new_out = pltpu.make_async_copy(new_ref, new_hbm, out_sem.at[0])
    new_out.start()
    d_normed = dot_t(d_logit.astype(BF16), gate_proj_ref[1])
    d_right = product(A1, D1)
    local[...] = left0
    d_left = turn(total(L1)).reshape(cells, hid)
    grad1 = entry(1, grad2, d_left, d_right, d_normed, hat1, inv1)

    d_hidden, d_logit = leave(0, grad1, gate0, update0, hid0, hid_inv0)
    share(D0, d_hidden.astype(BF16).reshape(t, t, hid))
    partials(D0, R0, False, arrive)
    d_normed = dot_t(d_logit.astype(BF16), gate_proj_ref[0])
    d_left = product(D0, B0)
    d_right = total(R0).reshape(cells, hid)
    grad0 = entry(0, grad1, d_left, d_right, d_normed, hat0, inv0)
    grad_ref[...] = grad0.reshape(t, t, ch)
    grad_out = pltpu.make_async_copy(grad_ref, grad_hbm, out_sem.at[1])
    grad_out.start()

    for copy in weight_copies:
        copy.wait_send()
    new_out.wait()
    for kind in range(A1, KINDS):
        for d in range(1, n):
            move(kind, after(here(kind), d), buf.at[kind, here(kind)]).wait_send()
    grad_out.wait()


def shards(
    n,
    n_chan,
    pair,
    window_start,
    residue_mask,
    in_gain,
    in_proj,
    gate_proj,
    out_gain,
    out_proj,
    cotangent,
):
    t, half, ch = cotangent.shape
    hid = out_proj.shape[1]
    turned = jnp.transpose(in_proj, (0, 2, 3, 1))
    hbm = pl.BlockSpec(memory_space=pltpu.HBM)
    smem = pl.BlockSpec(memory_space=pltpu.SMEM)
    return pl.pallas_call(
        functools.partial(kernel, n, n_chan),
        out_shape=(
            jax.ShapeDtypeStruct((t, half, ch), BF16),
            jax.ShapeDtypeStruct((t, half, ch), F32),
        ),
        in_specs=[hbm, smem] + [hbm] * 7,
        out_specs=(hbm, hbm),
        scratch_shapes=[
            pltpu.VMEM((t, half, ch), BF16),
            pltpu.VMEM((t, half, ch), F32),
            pltpu.VMEM((t, half, ch), BF16),
            pltpu.SMEM(residue_mask.shape, jnp.int32),
            pltpu.VMEM(in_gain.shape, F32),
            pltpu.VMEM(gate_proj.shape, BF16),
            pltpu.VMEM(out_gain.shape, F32),
            pltpu.VMEM(out_proj.shape, BF16),
            pltpu.VMEM((t, half, ch), BF16),
            pltpu.SemaphoreType.DMA((8,)),
            pltpu.SemaphoreType.DMA((2,)),
            pltpu.VMEM((KINDS, n, t, t, hid), BF16),
            pltpu.VMEM((R0 + 1 - H0, n, t, t, hid), BF16),
            pltpu.VMEM((2, 4, hid, ch), BF16),
            pltpu.VMEM((t, t, ch), F32),
            pltpu.VMEM((t, t, ch), F32),
            pltpu.VMEM((t, t, hid), F32),
            pltpu.VMEM((t, t, hid), F32),
            pltpu.VMEM((t, t, hid), F32),
            pltpu.VMEM((2, t * t, 4 * hid), F32),
            pltpu.VMEM((t * t, 4 * hid), BF16),
            pltpu.SemaphoreType.DMA((KINDS, n)),
            pltpu.SemaphoreType.DMA((KINDS, n)),
            pltpu.SemaphoreType.DMA((2, n_chan)),
            pltpu.SemaphoreType.DMA((2, n_chan)),
        ],
        compiler_params=pltpu.CompilerParams(
            collective_id=0, has_side_effects=True, vmem_limit_bytes=64 * 1024 * 1024
        ),
    )(pair, window_start, residue_mask, in_gain, turned, gate_proj, out_gain, out_proj, cotangent)


def solution(mesh):
    n = mesh.shape["row"]
    n_chan = mesh.shape["chan"]
    assert n == mesh.shape["col"] * n_chan
    placed = (
        P(("grp", "row"), "col", None),
        P("grp"),
        P("grp"),
        P(),
        P(None, None, None, "chan"),
        P(),
        P(),
        P(),
        P(("grp", "row"), ("col", "chan"), None),
    )
    out = P(("grp", "row"), ("col", "chan"), None)
    return jax.shard_map(
        functools.partial(shards, n, n_chan),
        mesh=mesh,
        in_specs=placed,
        out_specs=(out, out),
        check_vma=False,
    )
```

```python
import functools

import jax
import jax.numpy as jnp
from jax import lax
from jax.experimental import pallas as pl
from jax.experimental.pallas import tpu as pltpu
from jax.sharding import PartitionSpec as P

F32 = jnp.float32
BF16 = jnp.bfloat16
MESH = pl.DeviceIdType.MESH

B0, A1, D1, D0, H0, H1, L1, R0, PAIR = range(9)
KINDS = 9
IN_ROW = (A1, D0, H0, L1)


def dot(a, b):
    return lax.dot_general(a, b, (((1,), (0,)), ((), ())), preferred_element_type=F32)


def dot_t(a, b):
    return lax.dot_general(a, b, (((1,), (1,)), ((), ())), preferred_element_type=F32)


def unit(x):
    center = x - jnp.mean(x, axis=-1, keepdims=True)
    inv = lax.rsqrt(jnp.mean(center * center, axis=-1, keepdims=True) + 1e-05)
    return center * inv, inv


def unit_back(hat, inv, d_hat):
    mean = jnp.mean(d_hat, axis=-1, keepdims=True)
    slope = jnp.mean(d_hat * hat, axis=-1, keepdims=True)
    return inv * (d_hat - mean - hat * slope)


def kernel(
    n,
    n_chan,
    pair_hbm,
    start_ref,
    residue_hbm,
    in_gain_hbm,
    in_proj_ref,
    gate_proj_hbm,
    out_gain_hbm,
    out_proj_hbm,
    cot_hbm,
    new_hbm,
    grad_hbm,
    new_ref,
    grad_ref,
    pair_ref,
    residue_ref,
    in_gain_ref,
    gate_proj_ref,
    out_gain_ref,
    out_proj_ref,
    cot_ref,
    load_sem,
    out_sem,
    buf,
    stage,
    weight,
    mask_ref,
    mask_other,
    lhs_ref,
    acc_ref,
    local,
    proj_ref,
    wide_ref,
    send_sem,
    recv_sem,
    weight_send,
    weight_recv,
):
    t = cot_ref.shape[0]
    ch = cot_ref.shape[2]
    hid = weight.shape[2]
    cells = t * t
    r = lax.axis_index("row")
    chan = lax.axis_index("chan")
    q = lax.axis_index("col") * n_chan + chan

    def peer(in_row, place):
        if in_row:
            return {"col": place // n_chan, "chan": lax.rem(place, n_chan)}
        return {"row": place}

    def here(kind):
        return q if kind in IN_ROW else r

    def after(place, d):
        return lax.rem(place + d, n)

    part = in_proj_ref.shape[2]
    mine = pl.ds(pl.multiple_of(chan * part, part), part)
    own = pl.ds(pl.multiple_of(chan * t, t), t)
    loads = [
        pltpu.make_async_copy(source, target, load_sem.at[place])
        for place, (source, target) in enumerate(
            (
                (pair_hbm.at[:, own, :], pair_ref),
                (in_proj_ref, weight.at[:, :, mine, :]),
                (in_gain_hbm, in_gain_ref),
                (residue_hbm, residue_ref),
                (gate_proj_hbm, gate_proj_ref),
                (out_gain_hbm, out_gain_ref),
                (out_proj_hbm, out_proj_ref),
                (cot_hbm, cot_ref),
            )
        )
    ]
    for load in loads:
        load.start()

    barrier = pltpu.get_barrier_semaphore()
    for in_row in (True, False):
        for d in range(1, n):
            pl.semaphore_signal(
                barrier,
                inc=1,
                device_id=peer(in_row, after(q if in_row else r, d)),
                device_id_type=MESH,
            )
    pl.semaphore_wait(barrier, 2 * (n - 1))

    def move(kind, place, source):
        return pltpu.make_async_remote_copy(
            src_ref=source,
            dst_ref=buf.at[kind, here(kind)],
            send_sem=send_sem.at[kind, place],
            recv_sem=recv_sem.at[kind, here(kind)],
            device_id=peer(kind in IN_ROW, place),
            device_id_type=MESH,
        )

    def share(kind, value):
        buf[kind, here(kind)] = value
        for d in range(1, n):
            move(kind, after(here(kind), d), buf.at[kind, here(kind)]).start()

    def arrive(kind, slot):
        copy = pltpu.make_async_remote_copy(
            src_ref=buf.at[kind, slot],
            dst_ref=buf.at[kind, slot],
            send_sem=send_sem.at[kind, slot],
            recv_sem=recv_sem.at[kind, slot],
            device_id=peer(kind in IN_ROW, slot),
            device_id_type=MESH,
        )
        pl.when(slot != here(kind))(copy.wait_recv)

    loads[0].wait()
    for d in range(1, n):
        move(PAIR, after(r, d), pair_ref).start()

    loads[1].wait()
    weight_copies = []
    for u in range(2):
        for d in range(1, n_chan):
            copy = pltpu.make_async_remote_copy(
                src_ref=weight.at[u, :, mine, :],
                dst_ref=weight.at[u, :, mine, :],
                send_sem=weight_send.at[u, d - 1],
                recv_sem=weight_recv.at[u, chan],
                device_id={"chan": lax.rem(chan + d, n_chan)},
                device_id_type=MESH,
            )
            copy.start()
            weight_copies.append(copy)
    for load in loads[2:]:
        load.wait()

    first = start_ref[0]
    rows = lax.broadcasted_iota(jnp.int32, (t, ch), 0)
    col_mask = jnp.zeros((t, ch), F32)
    for j in range(t):
        value = residue_ref[first + q * t + j].astype(F32)
        col_mask = jnp.where(rows == j, value, col_mask)
    for i in range(t):
        mask_ref[i] = col_mask * residue_ref[first + r * t + i].astype(F32)

    def wait_weight(u):
        for d in range(1, n_chan):
            other = lax.rem(chan + d, n_chan)
            theirs = pl.ds(pl.multiple_of(other * part, part), part)
            pltpu.make_async_remote_copy(
                src_ref=weight.at[u, :, theirs, :],
                dst_ref=weight.at[u, :, theirs, :],
                send_sem=weight_send.at[u, d - 1],
                recv_sem=weight_recv.at[u, other],
                device_id={"chan": other},
                device_id_type=MESH,
            ).wait_recv()

    def enter(u, x):
        hat, inv = unit(x)
        return hat, inv, (hat * in_gain_ref[u : u + 1, :]).astype(BF16)

    def gated(u, normed, side):
        low, middle, high = side * hid, (side + 1) * hid, (side + 2) * hid
        wide = weight[u, side : side + 2].reshape(2 * hid, ch)
        proj_ref[u, :, low:high] = dot_t(normed, wide)
        mask = mask_ref[...].reshape(cells, ch)
        value = jax.nn.sigmoid(proj_ref[u, :, low:middle]) * proj_ref[u, :, middle:high] * mask
        return value.astype(BF16).reshape(t, t, hid)

    def project_other(kind, s):
        @pl.when(s != r)
        def _():
            arrive(PAIR, s)
            normed = enter(0, buf[PAIR, s].astype(F32).reshape(cells, ch))[2]
            both = dot_t(normed, weight[0, 2:4].reshape(2 * hid, ch))
            for i in range(t):
                mask_other[i] = col_mask * residue_ref[first + s * t + i].astype(F32)
            mask = mask_other[...].reshape(cells, ch)
            value = jax.nn.sigmoid(both[:, :hid]) * both[:, hid:] * mask
            buf[kind, s] = value.astype(BF16).reshape(t, t, hid)

    def gate_of(u, normed):
        return jax.nn.sigmoid(dot(normed, gate_proj_ref[u]))

    def multiply(left_major, right_of):
        for low in range(0, t, 8):
            acc = acc_ref[low : low + 8]
            for k in range(t):
                if left_major:
                    left = lhs_ref[low : low + 8, k : k + 1, :]
                else:
                    left = lhs_ref[k, low : low + 8, :].reshape(8, 1, hid)
                acc = acc + left * right_of(k)[None]
            acc_ref[low : low + 8] = acc

    def product(left_kind, right_kind):
        acc_ref[...] = jnp.zeros_like(acc_ref)

        def body(s, carry):
            lhs_ref[...] = buf[left_kind, s].astype(F32)
            multiply(True, lambda k: buf[right_kind, s, k].astype(F32))
            return carry

        lax.fori_loop(0, n, body, 0)
        return acc_ref[...].reshape(cells, hid)

    def partials(kind, out_kind, left_major, fetch):
        def body(d, carry):
            s = after(here(kind), n - d)
            fetch(kind, s)
            lhs_ref[...] = buf[kind, s].astype(F32)
            acc_ref[...] = jnp.zeros_like(acc_ref)
            multiply(left_major, lambda k: local[k])
            out = stage.at[out_kind - H0, s]
            out[...] = acc_ref[...].astype(BF16)

            @pl.when(s != here(out_kind))
            def _():
                move(out_kind, s, out).start()

            @pl.when(s == here(out_kind))
            def _():
                buf[out_kind, s] = acc_ref[...].astype(BF16)

            return carry

        lax.fori_loop(0, n, body, 0)

    def total(kind):
        acc_ref[...] = jnp.zeros_like(acc_ref)

        def body(d, carry):
            s = after(here(kind), n - d)
            arrive(kind, s)
            acc_ref[...] += buf[kind, s].astype(F32)
            return carry

        lax.fori_loop(0, n, body, 0)
        return acc_ref[...]

    def turn(value):
        return jnp.swapaxes(value.reshape(t, t, hid), 0, 1)

    def finish(u, hidden, x, gate):
        hat, inv = unit(hidden)
        scaled = (hat * out_gain_ref[u : u + 1, :]).astype(BF16)
        update = dot(scaled, out_proj_ref[u])
        return hat, inv, update, x + gate * update

    def leave(u, grad, gate, update, hat, inv):
        d_update = grad * gate
        d_logit = d_update * update * (1.0 - gate)
        d_scaled = dot_t(d_update.astype(BF16), out_proj_ref[u])
        d_hidden = unit_back(hat, inv, d_scaled * out_gain_ref[u : u + 1, :])
        return d_hidden, d_logit

    def entry(u, grad, d_left, d_right, d_normed, hat, inv):
        mask = mask_ref[...].reshape(cells, ch)
        for side, value in ((0, d_left * mask), (2, d_right * mask)):
            gate = jax.nn.sigmoid(proj_ref[u, :, side * hid : (side + 1) * hid])
            held = proj_ref[u, :, (side + 1) * hid : (side + 2) * hid]
            slope = value * gate
            wide_ref[:, side * hid : (side + 1) * hid] = (slope * held * (1.0 - gate)).astype(BF16)
            wide_ref[:, (side + 1) * hid : (side + 2) * hid] = slope.astype(BF16)
        d_entry = dot(wide_ref[...], weight[u].reshape(4 * hid, ch))
        return grad + unit_back(hat, inv, (d_entry + d_normed) * in_gain_ref[u : u + 1, :])

    x0 = pair_ref[...].astype(F32).reshape(cells, ch)
    hat0, inv0, normed0 = enter(0, x0)
    wait_weight(0)
    buf[B0, r] = gated(0, normed0, 2)
    left0 = gated(0, normed0, 0).astype(F32)
    local[...] = turn(left0)
    partials(B0, H0, True, project_other)
    gate0 = gate_of(0, normed0)
    hidden0 = turn(total(H0)).reshape(cells, hid).astype(BF16).astype(F32)
    hid0, hid_inv0, update0, middle = finish(0, hidden0, x0, gate0)
    x1 = middle.astype(BF16).astype(F32)

    hat1, inv1, normed1 = enter(1, x1)
    wait_weight(1)
    share(A1, gated(1, normed1, 0))
    right1 = gated(1, normed1, 2).astype(F32)
    local[...] = right1
    partials(A1, H1, False, arrive)
    gate1 = gate_of(1, normed1)
    local[...] = turn(right1)
    hidden1 = total(H1).reshape(cells, hid).astype(BF16).astype(F32)
    hid1, hid_inv1, update1, final = finish(1, hidden1, x1, gate1)

    grad2 = cot_ref[...].astype(F32).reshape(cells, ch)
    d_hidden, d_logit = leave(1, grad2, gate1, update1, hid1, hid_inv1)
    share(D1, d_hidden.astype(BF16).reshape(t, t, hid))
    partials(D1, L1, True, arrive)
    new_ref[...] = final.astype(BF16).reshape(t, t, ch)
    new_out = pltpu.make_async_copy(new_ref, new_hbm, out_sem.at[0])
    new_out.start()
    d_normed = dot_t(d_logit.astype(BF16), gate_proj_ref[1])
    d_right = product(A1, D1)
    local[...] = left0
    d_left = turn(total(L1)).reshape(cells, hid)
    grad1 = entry(1, grad2, d_left, d_right, d_normed, hat1, inv1)

    d_hidden, d_logit = leave(0, grad1, gate0, update0, hid0, hid_inv0)
    share(D0, d_hidden.astype(BF16).reshape(t, t, hid))
    partials(D0, R0, False, arrive)
    d_normed = dot_t(d_logit.astype(BF16), gate_proj_ref[0])
    d_left = product(D0, B0)
    d_right = total(R0).reshape(cells, hid)
    grad0 = entry(0, grad1, d_left, d_right, d_normed, hat0, inv0)
    grad_ref[...] = grad0.reshape(t, t, ch)
    grad_out = pltpu.make_async_copy(grad_ref, grad_hbm, out_sem.at[1])
    grad_out.start()

    for copy in weight_copies:
        copy.wait_send()
    new_out.wait()
    for kind in range(A1, KINDS):
        for d in range(1, n):
            move(kind, after(here(kind), d), buf.at[kind, here(kind)]).wait_send()
    grad_out.wait()


def shards(
    n,
    n_chan,
    pair,
    window_start,
    residue_mask,
    in_gain,
    in_proj,
    gate_proj,
    out_gain,
    out_proj,
    cotangent,
):
    t, half, ch = cotangent.shape
    hid = out_proj.shape[1]
    turned = jnp.transpose(in_proj, (0, 2, 3, 1))
    hbm = pl.BlockSpec(memory_space=pltpu.HBM)
    smem = pl.BlockSpec(memory_space=pltpu.SMEM)
    return pl.pallas_call(
        functools.partial(kernel, n, n_chan),
        out_shape=(
            jax.ShapeDtypeStruct((t, half, ch), BF16),
            jax.ShapeDtypeStruct((t, half, ch), F32),
        ),
        in_specs=[hbm, smem] + [hbm] * 7,
        out_specs=(hbm, hbm),
        scratch_shapes=[
            pltpu.VMEM((t, half, ch), BF16),
            pltpu.VMEM((t, half, ch), F32),
            pltpu.VMEM((t, half, ch), BF16),
            pltpu.SMEM(residue_mask.shape, jnp.int32),
            pltpu.VMEM(in_gain.shape, F32),
            pltpu.VMEM(gate_proj.shape, BF16),
            pltpu.VMEM(out_gain.shape, F32),
            pltpu.VMEM(out_proj.shape, BF16),
            pltpu.VMEM((t, half, ch), BF16),
            pltpu.SemaphoreType.DMA((8,)),
            pltpu.SemaphoreType.DMA((2,)),
            pltpu.VMEM((KINDS, n, t, t, hid), BF16),
            pltpu.VMEM((R0 + 1 - H0, n, t, t, hid), BF16),
            pltpu.VMEM((2, 4, hid, ch), BF16),
            pltpu.VMEM((t, t, ch), F32),
            pltpu.VMEM((t, t, ch), F32),
            pltpu.VMEM((t, t, hid), F32),
            pltpu.VMEM((t, t, hid), F32),
            pltpu.VMEM((t, t, hid), F32),
            pltpu.VMEM((2, t * t, 4 * hid), F32),
            pltpu.VMEM((t * t, 4 * hid), BF16),
            pltpu.SemaphoreType.DMA((KINDS, n)),
            pltpu.SemaphoreType.DMA((KINDS, n)),
            pltpu.SemaphoreType.DMA((2, n_chan)),
            pltpu.SemaphoreType.DMA((2, n_chan)),
        ],
        compiler_params=pltpu.CompilerParams(
            collective_id=0, has_side_effects=True, vmem_limit_bytes=64 * 1024 * 1024
        ),
    )(pair, window_start, residue_mask, in_gain, turned, gate_proj, out_gain, out_proj, cotangent)


def solution(mesh):
    n = mesh.shape["row"]
    n_chan = mesh.shape["chan"]
    assert n == mesh.shape["col"] * n_chan
    placed = (
        P(("grp", "row"), "col", None),
        P("grp"),
        P("grp"),
        P(),
        P(None, None, None, "chan"),
        P(),
        P(),
        P(),
        P(("grp", "row"), ("col", "chan"), None),
    )
    out = P(("grp", "row"), ("col", "chan"), None)
    return jax.shard_map(
        functools.partial(shards, n, n_chan),
        mesh=mesh,
        in_specs=placed,
        out_specs=(out, out),
        check_vma=False,
    )
```
